256 devices in a mesh: gx: 8 (over y, core), gy: 32 (over x, z).
Axes of the slice: x: 4, y: 4, z: 8, core: 2. Of those that a mesh axis runs over, the one named last changes fastest.
Arguments:
- mode_fields: float32 [64, 512, 1024], P(None, 'gy', 'gx'), may hold values from -8 to 8
- mean_field: float32 [512, 1024], P('gy', 'gx'), may hold values from 0.5 to 2
- coefficients: float32 [64, 131072], P(None, ('gx', 'gy')), may hold values from -40 to 40
Outputs:
- new_modes: float32 [64, 512, 1024], P(None, 'gy', 'gx')
- new_mean: float32 [512, 1024], P('gy', 'gx')
- new_coefficients: float32 [64, 131072], P(None, ('gx', 'gy'))
The draws below stay inside these ranges and needn't reach their ends.
All inputs are finite; a program needn't handle non-finite values.
Results may differ from the reference program's by a relative error of at most 0.0003.
Values sent between devices are 32-bit elements; how exact they have to be, the bound alone decides.
A program may use at most 128 MiB of HBM per device.

```python
import jax
import jax.numpy as jnp
from jax import lax

M = 64
NS_ITERS = 6
NX = 1024
NY = 512
R = 131072


def draw_mode_fields(key, part):
    subkeys = jax.random.split(key, 4)
    base_count = max(M // 4, 2)
    offsets = jax.random.uniform(subkeys[0], (M, 1, 1), jnp.float32, -0.7, 0.7)
    mixing = jax.random.normal(subkeys[1], (M, base_count), jnp.float32) / jnp.sqrt(jnp.float32(base_count))
    white_parts = jax.random.normal(subkeys[2], (base_count, NY, NX), jnp.float32)
    noise_part = jax.random.normal(subkeys[3], (M, NY, NX), jnp.float32)
    smooth = (white_parts + jnp.roll(white_parts, 1, axis=2) + jnp.roll(white_parts, 1, axis=1)) / jnp.sqrt(jnp.float32(3.0))
    base_fields = (smooth * smooth - 1.0) / jnp.sqrt(jnp.float32(2.0))
    mixture = jnp.dot(mixing, base_fields.reshape(base_count, NY * NX), precision=lax.Precision.HIGHEST).reshape(M, NY, NX)
    values = offsets + (0.85 * mixture + 0.6 * noise_part)
    return jnp.clip(values, -8.0, 8.0)


def draw_coefficients(key, part):
    subkeys = jax.random.split(key, 6)
    scales = jnp.exp(jax.random.uniform(subkeys[0], (M, 1), jnp.float32, -0.6931, 0.6931))
    skewness = jax.random.uniform(subkeys[1], (M, 1), jnp.float32, -0.3, 0.3)
    shared = jax.random.uniform(subkeys[2], (M, 1), jnp.float32, -0.3, 0.3)
    drifts = jax.random.uniform(subkeys[3], (M, 1), jnp.float32, -1.0, 1.0)
    private = jax.random.normal(subkeys[4], (M, R), jnp.float32)
    common = jax.random.normal(subkeys[5], (1, R), jnp.float32)
    position_ramp = 1.0 + 2.0 * jnp.arange(R, dtype=jnp.float32) / R
    values = scales * (private + skewness * (private * private - 1.0) + shared * (common * common - 1.0))
    values = values + drifts * scales * position_ramp[None, :]
    return jnp.clip(values, -40.0, 40.0)


def shard_levels(rng, shape, cuts, least, top_value):
    gain, own = 1.0, jax.random.fold_in(rng, 6)
    for axis_at, parts in cuts:
        steps = jnp.exp(jax.random.uniform(jax.random.fold_in(own, axis_at), (parts,), jnp.float32, least / len(cuts), top_value / len(cuts)))
        gain = gain * jnp.repeat(steps, shape[axis_at] // parts).reshape([-1 if axis == axis_at else 1 for axis in range(len(shape))])
    return gain


def setup_inputs(seed: int = 0) -> dict:
    key_of = jax.random.split(jax.random.key(seed), 4)
    return {
        "mode_fields": draw_mode_fields(jax.random.fold_in(key_of[3], 71), 0),
        "mean_field": jnp.clip(0.5 + 1.5 * jax.random.uniform(key_of[1], (NY, NX), jnp.float32) ** shard_levels(key_of[1], (NY, NX), ((0, 32), (1, 8)), -0.2, 0.2), 0.5, 2.0),
        "coefficients": draw_coefficients(jax.random.fold_in(key_of[3], 71), 0),
    }


TIME_STEP = 0.02
VISCOSITY = 0.25
PRECISE = lax.Precision.HIGHEST

def upwind(values):
    return 2.0 * values - jnp.roll(values, 1, axis=-1) - jnp.roll(values, 1, axis=-2)

def laplacian(values):
    beside_all = jnp.roll(values, 1, axis=-1) + jnp.roll(values, -1, axis=-1)
    beside_all = beside_all + jnp.roll(values, 1, axis=-2) + jnp.roll(values, -1, axis=-2)
    return beside_all - 4.0 * values

def inverse_root(covariance):
    identity = jnp.eye(covariance.shape[0], dtype=jnp.float32)
    scaling = jnp.sqrt(jnp.sum(covariance * covariance) + 1e-06)
    current = covariance / scaling
    inverse = identity
    for iteration in range(NS_ITERS):
        middle = 0.5 * (3.0 * identity - jnp.dot(inverse, current, precision=PRECISE))
        current = jnp.dot(current, middle, precision=PRECISE)
        inverse = jnp.dot(middle, inverse, precision=PRECISE)
    return inverse / jnp.sqrt(scaling)

def reference(mode_fields, mean_field, coefficients):
    cell_count = NX * NY
    samples = coefficients.shape[1]
    flattened = mode_fields.reshape(M, cell_count)
    gradient = upwind(mode_fields).reshape(M, cell_count)
    smoothed = laplacian(mode_fields).reshape(M, cell_count)
    mean_flat = mean_field.reshape(cell_count)
    mean_gradient = upwind(mean_field).reshape(cell_count)
    mean_smooth = laplacian(mean_field).reshape(cell_count)
    linear = -mean_flat * gradient - flattened * mean_gradient + VISCOSITY * smoothed
    coupling = jnp.dot(flattened, linear.T, precision=PRECISE) / cell_count

    def triad_row(position):
        product = flattened[position] * gradient
        return -jnp.dot(product, flattened.T, precision=PRECISE) / cell_count
    triads = lax.map(triad_row, jnp.arange(M, dtype=jnp.int32))
    sample_mean = lax.optimization_barrier(jnp.sum(coefficients, axis=1, keepdims=True)) / samples
    centered = coefficients - sample_mean
    covariance = jnp.dot(centered, centered.T, precision=PRECISE) / samples

    def third_row(position):
        return jnp.dot(centered[position] * centered, centered.T, precision=PRECISE) / samples
    third_moment = lax.map(third_row, jnp.arange(M, dtype=jnp.int32))

    def quad_step(total, position):
        weights = centered[position] * centered - covariance[position][:, None]
        return (total + jnp.dot(triads[position].T, weights, precision=PRECISE), None)
    quadratic, unused = lax.scan(quad_step, jnp.zeros((M, samples), jnp.float32), jnp.arange(M, dtype=jnp.int32))
    new_coefficients = centered + TIME_STEP * (jnp.dot(coupling, centered, precision=PRECISE) + quadratic)
    weighted = jnp.dot(covariance.T, flattened, precision=PRECISE)
    new_mean = mean_flat + TIME_STEP * (-mean_flat * mean_gradient + VISCOSITY * mean_smooth - lax.optimization_barrier(jnp.sum(weighted * gradient, axis=0)))

    def force_step(total, position):
        product = flattened[position] * gradient
        return (total + jnp.dot(third_moment[:, position, :], product, precision=PRECISE), None)
    moment_term, unused = lax.scan(force_step, jnp.zeros((M, cell_count), jnp.float32), jnp.arange(M, dtype=jnp.int32))
    forcing = jnp.dot(covariance, linear, precision=PRECISE) - moment_term
    projection = jnp.dot(forcing, flattened.T, precision=PRECISE) / cell_count
    residual = forcing - jnp.dot(projection, flattened, precision=PRECISE)
    half_power = inverse_root(covariance)
    weighting = jnp.dot(half_power, half_power, precision=PRECISE)
    stepped = flattened + TIME_STEP * jnp.dot(weighting, residual, precision=PRECISE)
    gram_matrix = jnp.dot(stepped, stepped.T, precision=PRECISE) / cell_count
    factor = jnp.linalg.cholesky(gram_matrix)
    new_modes = lax.linalg.triangular_solve(factor, stepped, left_side=True, lower=True)
    return (new_modes.reshape(M, NY, NX), new_mean.reshape(NY, NX), new_coefficients)
```

```python
import functools

import jax
import jax.numpy as jnp
from jax import lax
from jax.experimental import pallas as pl
from jax.experimental.pallas import tpu as pltpu
from jax.sharding import PartitionSpec as P

NS_ITERS = 6
TIME_STEP = 0.02
VISCOSITY = 0.25
M = 64
F32 = jnp.float32
BF16 = jnp.bfloat16
HIGHEST = lax.Precision.HIGHEST
MESH = pl.DeviceIdType.MESH
SIZES = {"c": 2, "y": 4, "x": 4, "z": 8}

BASES = [sum(8 * (M - 8 * b) for b in range(block)) for block in range(9)]
PAIRS = BASES[8]
HALF = PAIRS // 2
GROUPS = ((0,), (1,), (2, 3), (4, 5, 6, 7))
SMALL = M // 2
ROWS = 1280


def coordinates():
    gx, gy = lax.axis_index("gx"), lax.axis_index("gy")
    return {"c": gx % 2, "y": gx // 2, "x": gy // 8, "z": gy % 8}


def group_size(axes):
    size = 1
    for axis in axes:
        size *= SIZES[axis]
    return size


def member_id(axes, member, place):
    place = dict(place)
    for axis in reversed(axes):
        place[axis] = member % SIZES[axis]
        member = member // SIZES[axis]
    return (place["y"] * 2 + place["c"], place["x"] * 8 + place["z"])


def own_member(axes, place):
    index = 0
    for axis in axes:
        index = index * SIZES[axis] + place[axis]
    return index


class AllReduce:
    def __init__(self, place, buffer, result, stages, refs):
        self.place, self.buffer, self.result = place, buffer, result
        self.last_up = len(stages)
        self.steps = []
        base, size = 0, buffer.shape[0]
        at = 0
        back = []
        for axes, scatter in stages:
            n = group_size(axes)
            piece = size // n if scatter else size
            self.steps.append(("up", axes, scatter, base, piece, refs[at : at + 3]))
            at += 3
            if scatter:
                back.append((axes, base, piece))
                base = base + own_member(axes, place) * piece
            size = piece
        for axes, start, piece in reversed(back):
            self.steps.append(("down", axes, False, start, piece, refs[at : at + 2]))
            at += 2
        self.started = 0
        self.finished = 0
        self.copies = []

    @staticmethod
    def scratch(rows, stages):
        shapes = []
        size = rows
        back = []
        for axes, scatter in stages:
            n = group_size(axes)
            size = size // n if scatter else size
            shapes += [pltpu.VMEM((n - 1, size, 128), F32)] + [pltpu.SemaphoreType.DMA((n - 1,))] * 2
            if scatter:
                back.append(axes)
        for axes in reversed(back):
            shapes += [pltpu.SemaphoreType.DMA((group_size(axes) - 1,))] * 2
        return shapes

    def start(self):
        kind, axes, scatter, base, piece, refs = self.steps[self.started]
        self.started += 1
        n, me = group_size(axes), own_member(axes, self.place)
        send, recv = refs[-2], refs[-1]
        self.copies = []
        for offset in range(1, n):
            member = (me + offset) % n
            if kind == "up":
                at = base + member * piece if scatter else base
                source = self.buffer.at[pl.ds(pl.multiple_of(at, 8), piece)]
                target = refs[0].at[offset - 1]
            else:
                source = self.result.at[pl.ds(pl.multiple_of(base + me * piece, 8), piece)]
                target = source
            copy = pltpu.make_async_remote_copy(
                src_ref=source,
                dst_ref=target,
                send_sem=send.at[offset - 1],
                recv_sem=recv.at[offset - 1],
                device_id=member_id(axes, member, self.place),
                device_id_type=MESH,
            )
            copy.start()
            self.copies.append(copy)

    def finish(self):
        kind, axes, scatter, base, piece, refs = self.steps[self.finished]
        self.finished += 1
        for copy in self.copies:
            copy.wait_recv()
        for copy in self.copies:
            copy.wait_send()
        if kind == "up":
            at = base + own_member(axes, self.place) * piece if scatter else base
            rows = pl.ds(pl.multiple_of(at, 8), piece)
            total = self.buffer[rows]
            for slot in range(group_size(axes) - 1):
                total = total + refs[0][slot]
            if self.finished == self.last_up:
                self.result[rows] = total
            else:
                self.buffer[rows] = total

    def advance(self):
        self.finish()
        if self.started < len(self.steps):
            self.start()

    def drain(self):
        while self.finished < len(self.steps):
            self.advance()


BIG = (("c", True), ("xy", True), ("z", False))
TINY = (("c", False), ("xy", False), ("z", False))
MID = (("c", True), ("xy", False), ("z", False))


def dot(left, right, precision=None):
    return jnp.dot(left, right, preferred_element_type=F32, precision=precision)


def dot_nt(left, right, precision=None):
    return lax.dot_general(
        left, right, (((1,), (1,)), ((), ())), preferred_element_type=F32, precision=precision
    )


def split(values):
    high = values.astype(BF16)
    return high, (values - high.astype(F32)).astype(BF16)


def stack4(values):
    high, low = split(values)
    return jnp.concatenate([high, high, low, low], axis=0)


def lanes_of(shape):
    return lax.broadcasted_iota(jnp.int32, shape, len(shape) - 1)


def high_low(doubled):
    high = doubled.astype(BF16).astype(F32)
    return jnp.where(lanes_of(doubled.shape) < M, high, doubled - high).astype(BF16)


def twice(values):
    return jnp.concatenate([values, values], axis=1)


def pair_rows(values, blocks):
    rows = []
    for block in blocks:
        others = values[8 * block :]
        for i in range(8 * block, 8 * block + 8):
            rows.append(values[i : i + 1] * others)
    return jnp.concatenate(rows, axis=0)


def add_pairs(total_ref, values, weights, first=False):
    for blocks in GROUPS:
        rows = slice(BASES[blocks[0]], BASES[blocks[-1] + 1])
        high, low = split(pair_rows(values, blocks))
        part = dot_nt(high, weights) + dot_nt(low, weights)
        if first:
            total_ref[rows] = part
        else:
            total_ref[rows] += part


def pack(total_ref, small, buffer_ref, scale):
    for at in range(0, HALF, 128):
        top = total_ref[at : at + 128]
        bottom = total_ref[HALF + at : HALF + at + 128]
        top = top + pltpu.roll(top, M, 1)
        bottom = bottom + pltpu.roll(bottom, M, 1)
        buffer_ref[at : at + 128] = jnp.where(lanes_of(top.shape) < M, top, bottom) * scale
    buffer_ref[HALF : HALF + SMALL] = (
        jnp.where(lanes_of((SMALL, 128)) < M, small[:SMALL], small[SMALL:]) * scale
    )
    buffer_ref[HALF + SMALL :] = jnp.zeros((ROWS - HALF - SMALL, 128), F32)


def unpack_rows(packed):
    turned = pltpu.roll(packed, M, 1)
    left = lanes_of(packed.shape) < M
    return jnp.where(left, packed, turned), jnp.where(left, turned, packed)


def unpack_small(packed):
    top, bottom = unpack_rows(packed)
    return jnp.concatenate([top, bottom], axis=0)


def expand(buffer_ref, pairs_ref, full_ref):
    for at in range(0, HALF, 128):
        top, bottom = unpack_rows(buffer_ref[at : at + 128])
        pairs_ref[at : at + 128] = top
        pairs_ref[HALF + at : HALF + at + 128] = bottom
    for i in range(M):
        block = i // 8
        count = M - 8 * block
        start = BASES[block] + (i - 8 * block) * count
        full_ref[i * M + 8 * block : (i + 1) * M] = pairs_ref[start : start + count]
        for below in range(block):
            stride = M - 8 * below
            start = BASES[below] + i - 8 * below
            full_ref[i * M + 8 * below : i * M + 8 * below + 8] = pairs_ref[
                pl.ds(start, 8, stride=stride), :
            ]


def contract(parts_ref, stacked, factors, total):
    for chunk in range(8):
        left = parts_ref[chunk * 512 : (chunk + 1) * 512]
        inner = dot(twice(left), stacked)
        for i in range(8):
            at = chunk * 8 + i
            total = total + inner[i * M : (i + 1) * M] * factors[at : at + 1]
    return total


def newton_schulz(covariance):
    row = lax.broadcasted_iota(jnp.int32, (M, M), 0)
    identity = jnp.where(row == lanes_of((M, M)), 1.0, 0.0).astype(F32)
    square = jnp.sum(jnp.sum(covariance * covariance, axis=1, keepdims=True), axis=0, keepdims=True)
    scaling = jnp.sqrt(square + 1e-06)
    current = covariance / scaling
    inverse = identity
    for iteration in range(NS_ITERS):
        middle = 0.5 * (3.0 * identity - dot(inverse, current, HIGHEST))
        current = dot(current, middle, HIGHEST)
        inverse = dot(middle, inverse, HIGHEST)
    half_power = inverse / jnp.sqrt(scaling)
    return dot(half_power, half_power, HIGHEST)


def inverse_factor(gram):
    row = lax.broadcasted_iota(jnp.int32, (M, 2 * M), 0)
    lane = lanes_of((M, 2 * M))
    table = jnp.where(lane < M, gram, jnp.where(lane - M == row, 1.0, 0.0))
    pivots = jnp.ones((M, 1), F32)
    column_row = lax.broadcasted_iota(jnp.int32, (M, 1), 0)
    for k in range(M):
        pivot_row = table[k : k + 1]
        pivot = pivot_row[:, k : k + 1]
        factor = jnp.where(column_row > k, table[:, k : k + 1] / pivot, 0.0)
        pivots = jnp.where(column_row == k, pivot, pivots)
        table = table - factor * pivot_row
    return table[:, M:] * lax.rsqrt(pivots)


def kernel(cells, samples, modes_ref, mean_ref, coef_ref, out_modes, out_mean, out_coef, *scratch):
    (field, grad, linear, force, centered, pair_sum, pairs, full_t, full_q,
     t_parts, q_parts, q_high, q_low, halo_send, halo_recv, halo_ssem, halo_rsem,
     mean_buf, t_buf, q_buf, gram_buf, t_all, q_all, gram_all) = scratch[:24]
    refs = scratch[24:]
    place = coordinates()
    gx, gy = lax.axis_index("gx"), lax.axis_index("gy")
    barrier = pltpu.get_barrier_semaphore()
    around = [((gx + 1) % 8, gy), ((gx + 7) % 8, gy), (gx, (gy + 1) % 32), (gx, (gy + 31) % 32)]
    count = 0
    for axes in ("c", "xy", "z"):
        n, me = group_size(axes), own_member(axes, place)
        for offset in range(1, n):
            pl.semaphore_signal(
                barrier, inc=1, device_id=member_id(axes, (me + offset) % n, place), device_id_type=MESH
            )
            count += 1
    for neighbour in around:
        pl.semaphore_signal(barrier, inc=1, device_id=neighbour, device_id_type=MESH)
        count += 1

    reducers = []
    at = 0
    for buffer, result, stages in (
        (mean_buf, mean_buf, TINY),
        (t_buf, t_all, BIG),
        (q_buf, q_all, BIG),
        (gram_buf, gram_all, MID),
    ):
        shapes = AllReduce.scratch(buffer.shape[0], stages)
        reducers.append(AllReduce(place, buffer, result, stages, refs[at : at + len(shapes)]))
        at += len(shapes)
    mean_sum, t_sum, q_sum, gram_sum = reducers

    eye = lax.broadcasted_iota(jnp.int32, (M, 128), 0) == lanes_of((M, 128))
    sums = jnp.sum(coef_ref[...], axis=1, keepdims=True)
    mean_buf[...] = jnp.broadcast_to(
        jnp.sum(jnp.where(eye, sums, 0.0), axis=0, keepdims=True), (8, 128)
    )

    rows = 72
    lane = lanes_of((rows, 128))
    first = jnp.zeros((rows, 128), F32)
    last = jnp.zeros((rows, 128), F32)
    for y in range(16):
        field[y, :M] = modes_ref[y]
        field[y, M:] = jnp.broadcast_to(mean_ref[y : y + 1], (8, 128))
        here = field[y]
        first = jnp.where(lane == y, pltpu.roll(here, y, 1) if y else here, first)
        last = jnp.where(lane == y, pltpu.roll(here, y + 1, 1), last)
        inner = 2.0 * here - jnp.where(lane == 0, 0.0, pltpu.roll(here, 1, 1))
        if y:
            inner = inner - field[y - 1]
        grad[y] = inner
    halo_send[0] = last
    halo_send[1] = first
    halo_send[2] = field[15]
    halo_send[3] = field[0]

    pl.semaphore_wait(barrier, count)
    mean_sum.start()
    halos = []
    for side in range(4):
        copy = pltpu.make_async_remote_copy(
            src_ref=halo_send.at[side],
            dst_ref=halo_recv.at[side],
            send_sem=halo_ssem.at[side],
            recv_sem=halo_rsem.at[side],
            device_id=around[side],
            device_id_type=MESH,
        )
        copy.start()
        halos.append(copy)

    def wide(ref, t):
        return jnp.concatenate([ref[2 * t, :M], ref[2 * t + 1, :M]], axis=1)

    def triad_step(t, carry):
        add_pairs(pair_sum, wide(field, t), jnp.concatenate(split(wide(grad, t)), axis=0))
        return carry

    pair_sum[...] = jnp.zeros(pair_sum.shape, F32)
    lax.fori_loop(0, 3, triad_step, 0)
    mean_sum.advance()
    lax.fori_loop(3, 8, triad_step, 0)

    for copy in halos:
        copy.wait_recv()
    for copy in halos:
        copy.wait_send()
    west, east, south, north = halo_recv[0], halo_recv[1], halo_recv[2], halo_recv[3]
    edge = jnp.concatenate([field[0, :M], first[:M]], axis=1)
    beyond = jnp.concatenate([south[:M], jnp.where(lane < 16, west, 0.0)[:M]], axis=1)
    add_pairs(pair_sum, edge, jnp.concatenate(split(-beyond), axis=0))
    coupling = jnp.zeros((M, 128), F32)
    for y in range(16):
        here = field[y]
        from_west = pltpu.roll(west, (128 - y) % 128, 1) if y else west
        from_east = pltpu.roll(east, 127 - y, 1)
        below = field[y - 1] if y else south
        above = field[y + 1] if y < 15 else north
        left = jnp.where(lane == 0, from_west, pltpu.roll(here, 1, 1))
        right = jnp.where(lane == 127, from_east, pltpu.roll(here, 127, 1))
        up = 2.0 * here - left - below
        lap = left + right + below + above - 4.0 * here
        grad[y] = up
        mean = mean_ref[y : y + 1]
        mean_up = up[M : M + 1]
        line = -mean * up[:M] - here[:M] * mean_up + VISCOSITY * lap[:M]
        linear[y] = line
        out_mean[y : y + 1] = mean + TIME_STEP * (-mean * mean_up + VISCOSITY * lap[M : M + 1])
        coupling = coupling + dot_nt(here[:M], jnp.concatenate([line, line], axis=0), HIGHEST)
    pack(pair_sum, -coupling, q_buf, -1.0 / cells)
    mean_sum.advance()
    q_sum.start()
    mean_sum.finish()

    sample_mean = jnp.sum(jnp.where(eye, mean_buf[0:1], 0.0), axis=1, keepdims=True) / samples
    centered[...] = coef_ref[...] - sample_mean
    for t in range(2):
        values = centered[:, 256 * t : 256 * t + 256]
        add_pairs(pair_sum, values, jnp.concatenate(split(values), axis=0), first=t == 0)
    values = centered[...]
    second = dot_nt(values, jnp.concatenate([values, values], axis=0), HIGHEST)
    pack(pair_sum, second, t_buf, 1.0 / samples)
    t_sum.start()
    q_sum.advance()
    t_sum.advance()
    q_sum.advance()
    t_sum.advance()
    q_sum.advance()
    t_sum.advance()
    q_sum.advance()
    t_sum.advance()
    q_sum.finish()
    t_sum.finish()

    covariance = unpack_small(t_all[HALF : HALF + SMALL])
    coupled = unpack_small(q_all[HALF : HALF + SMALL])
    expand(t_all, pairs, full_t)
    expand(q_all, pairs, full_q)
    constant = jnp.zeros((M, 128), F32)
    for j in range(M):
        at = slice(j * M, (j + 1) * M)
        t_parts[at] = high_low(full_t[at])
        q_values = full_q[at]
        high, low = split(q_values)
        q_high[at] = high
        q_low[at] = low
        q_parts[at] = high_low(q_values)
        constant = constant + q_values * covariance[j : j + 1]
    constant = jnp.sum(jnp.where(lanes_of((M, 128)) < M, constant, 0.0), axis=1, keepdims=True)
    covariance_parts = twice(high_low(covariance))

    def force_step(t, carry):
        modes = wide(field, t)
        slope = wide(grad, t)
        stacked = stack4(modes)
        line = wide(linear, t)
        moment = contract(t_parts, stacked, slope, jnp.zeros((M, 256), F32))
        forcing = dot(covariance_parts, stack4(line)) - moment
        force[2 * t] = forcing[:, :128]
        force[2 * t + 1] = forcing[:, 128:]
        mixed = dot(covariance_parts, stacked) * slope
        row = TIME_STEP * jnp.sum(mixed, axis=0, keepdims=True)
        out_mean[pl.ds(2 * t, 1)] += -row[:, :128]
        out_mean[pl.ds(2 * t + 1, 1)] += -row[:, 128:]
        return carry

    lax.fori_loop(0, 8, force_step, 0)

    def project_step(k, total):
        at = pl.ds(pl.multiple_of(k * M, M), M)
        left = twice(t_parts[at])
        right = jnp.concatenate([q_high[at], q_low[at]], axis=1)
        return total + dot_nt(left, jnp.concatenate([right, right], axis=0))

    projection = lax.fori_loop(0, M, project_step, jnp.zeros((M, 128), F32))
    half = jnp.where(lanes_of((M, 128)) < M, covariance, 0.0)
    projection = projection + dot_nt(half, jnp.concatenate([coupled, coupled], axis=0), HIGHEST)
    weighting = newton_schulz(covariance[:, :M])
    weighting_parts = twice(high_low(twice(weighting)))
    projection_parts = twice(high_low(projection))

    def step_step(t, total):
        modes = wide(field, t)
        residual = wide(force, t) - dot(projection_parts, stack4(modes))
        stepped = modes + TIME_STEP * dot(weighting_parts, stack4(residual))
        force[2 * t] = stepped[:, :128]
        force[2 * t + 1] = stepped[:, 128:]
        return total + dot_nt(stepped, jnp.concatenate([stepped, stepped], axis=0), HIGHEST)

    gram = lax.fori_loop(0, 8, step_step, jnp.zeros((M, 128), F32))
    gram_buf[...] = jnp.where(lanes_of((SMALL, 128)) < M, gram[:SMALL], gram[SMALL:]) * (1.0 / cells)
    gram_sum.start()

    coupled_parts = twice(high_low(coupled))

    for t in range(2):
        values = centered[:, 256 * t : 256 * t + 256]
        stacked = stack4(values)
        total = contract(q_parts, stacked, values, dot(coupled_parts, stacked)) - constant
        out_coef[:, 256 * t : 256 * t + 256] = values + TIME_STEP * total

    gram_sum.drain()
    inverse = inverse_factor(unpack_small(gram_all[...]))

    def final_step(y, carry):
        out_modes[y] = dot(inverse, force[y], HIGHEST)
        return carry

    lax.fori_loop(0, 16, final_step, 0)


def per_device(mode_fields, mean_field, coefficients):
    devices = lax.axis_size("gx") * lax.axis_size("gy")
    cells = mode_fields.shape[1] * mode_fields.shape[2] * devices
    samples = coefficients.shape[1] * devices
    scratch = [
        pltpu.VMEM((16, 72, 128), F32),
        pltpu.VMEM((16, 72, 128), F32),
        pltpu.VMEM((16, M, 128), F32),
        pltpu.VMEM((16, M, 128), F32),
        pltpu.VMEM((M, 512), F32),
        pltpu.VMEM((PAIRS, 128), F32),
        pltpu.VMEM((PAIRS, 128), F32),
        pltpu.VMEM((M * M, 128), F32),
        pltpu.VMEM((M * M, 128), F32),
        pltpu.VMEM((M * M, 128), BF16),
        pltpu.VMEM((M * M, 128), BF16),
        pltpu.VMEM((M * M, 128), BF16),
        pltpu.VMEM((M * M, 128), BF16),
        pltpu.VMEM((4, 72, 128), F32),
        pltpu.VMEM((4, 72, 128), F32),
        pltpu.SemaphoreType.DMA((4,)),
        pltpu.SemaphoreType.DMA((4,)),
        pltpu.VMEM((8, 128), F32),
        pltpu.VMEM((ROWS, 128), F32),
        pltpu.VMEM((ROWS, 128), F32),
        pltpu.VMEM((SMALL, 128), F32),
        pltpu.VMEM((ROWS, 128), F32),
        pltpu.VMEM((ROWS, 128), F32),
        pltpu.VMEM((SMALL, 128), F32),
    ]
    for rows, stages in ((8, TINY), (ROWS, BIG), (ROWS, BIG), (SMALL, MID)):
        scratch += AllReduce.scratch(rows, stages)
    whole = pl.BlockSpec(memory_space=pltpu.VMEM)
    fields, new_mean, new_coefficients = pl.pallas_call(
        functools.partial(kernel, cells, samples),
        out_shape=(
            jax.ShapeDtypeStruct((16, M, 128), F32),
            jax.ShapeDtypeStruct(mean_field.shape, F32),
            jax.ShapeDtypeStruct(coefficients.shape, F32),
        ),
        in_specs=[whole] * 3,
        out_specs=(whole,) * 3,
        scratch_shapes=scratch,
        compiler_params=pltpu.CompilerParams(
            collective_id=0, has_side_effects=True, vmem_limit_bytes=56 * 2**20
        ),
    )(jnp.transpose(mode_fields, (1, 0, 2)), mean_field, coefficients)
    return jnp.transpose(fields, (1, 0, 2)), new_mean, new_coefficients


def solution(mesh):
    placed = (P(None, "gy", "gx"), P("gy", "gx"), P(None, ("gx", "gy")))
    return jax.shard_map(
        per_device, mesh=mesh, in_specs=placed, out_specs=placed, check_vma=False
    )
```

```python
import functools

import jax
import jax.numpy as jnp
from jax import lax
from jax.experimental import pallas as pl
from jax.experimental.pallas import tpu as pltpu
from jax.sharding import PartitionSpec as P

NS_ITERS = 6
TIME_STEP = 0.02
VISCOSITY = 0.25
M = 64
F32 = jnp.float32
BF16 = jnp.bfloat16
HIGHEST = lax.Precision.HIGHEST
MESH = pl.DeviceIdType.MESH
SIZES = {"c": 2, "y": 4, "x": 4, "z": 8}

BASES = [sum(8 * (M - 8 * b) for b in range(block)) for block in range(9)]
PAIRS = BASES[8]
HALF = PAIRS // 2
GROUPS = ((0,), (1,), (2, 3), (4, 5, 6, 7))
SMALL = M // 2
ROWS = 1280


def coordinates():
    gx, gy = lax.axis_index("gx"), lax.axis_index("gy")
    return {"c": gx % 2, "y": gx // 2, "x": gy // 8, "z": gy % 8}


def group_size(axes):
    size = 1
    for axis in axes:
        size *= SIZES[axis]
    return size


def member_id(axes, member, place):
    place = dict(place)
    for axis in reversed(axes):
        place[axis] = member % SIZES[axis]
        member = member // SIZES[axis]
    return (place["y"] * 2 + place["c"], place["x"] * 8 + place["z"])


def own_member(axes, place):
    index = 0
    for axis in axes:
        index = index * SIZES[axis] + place[axis]
    return index


class AllReduce:
    def __init__(self, place, buffer, result, stages, refs):
        self.place, self.buffer, self.result = place, buffer, result
        self.last_up = len(stages)
        self.steps = []
        base, size = 0, buffer.shape[0]
        at = 0
        back = []
        for axes, scatter in stages:
            n = group_size(axes)
            piece = size // n if scatter else size
            self.steps.append(("up", axes, scatter, base, piece, refs[at : at + 3]))
            at += 3
            if scatter:
                back.append((axes, base, piece))
                base = base + own_member(axes, place) * piece
            size = piece
        for axes, start, piece in reversed(back):
            self.steps.append(("down", axes, False, start, piece, refs[at : at + 2]))
            at += 2
        self.started = 0
        self.finished = 0
        self.copies = []

    @staticmethod
    def scratch(rows, stages):
        shapes = []
        size = rows
        back = []
        for axes, scatter in stages:
            n = group_size(axes)
            size = size // n if scatter else size
            shapes += [pltpu.VMEM((n - 1, size, 128), F32)] + [pltpu.SemaphoreType.DMA((n - 1,))] * 2
            if scatter:
                back.append(axes)
        for axes in reversed(back):
            shapes += [pltpu.SemaphoreType.DMA((group_size(axes) - 1,))] * 2
        return shapes

    def start(self):
        kind, axes, scatter, base, piece, refs = self.steps[self.started]
        self.started += 1
        n, me = group_size(axes), own_member(axes, self.place)
        send, recv = refs[-2], refs[-1]
        self.copies = []
        for offset in range(1, n):
            member = (me + offset) % n
            if kind == "up":
                at = base + member * piece if scatter else base
                source = self.buffer.at[pl.ds(pl.multiple_of(at, 8), piece)]
                target = refs[0].at[offset - 1]
            else:
                source = self.result.at[pl.ds(pl.multiple_of(base + me * piece, 8), piece)]
                target = source
            copy = pltpu.make_async_remote_copy(
                src_ref=source,
                dst_ref=target,
                send_sem=send.at[offset - 1],
                recv_sem=recv.at[offset - 1],
                device_id=member_id(axes, member, self.place),
                device_id_type=MESH,
            )
            copy.start()
            self.copies.append(copy)

    def finish(self):
        kind, axes, scatter, base, piece, refs = self.steps[self.finished]
        self.finished += 1
        for copy in self.copies:
            copy.wait_recv()
        for copy in self.copies:
            copy.wait_send()
        if kind == "up":
            at = base + own_member(axes, self.place) * piece if scatter else base
            rows = pl.ds(pl.multiple_of(at, 8), piece)
            total = self.buffer[rows]
            for slot in range(group_size(axes) - 1):
                total = total + refs[0][slot]
            if self.finished == self.last_up:
                self.result[rows] = total
            else:
                self.buffer[rows] = total

    def advance(self):
        self.finish()
        if self.started < len(self.steps):
            self.start()

    def drain(self):
        while self.finished < len(self.steps):
            self.advance()


BIG = (("c", True), ("xy", True), ("z", False))
TINY = (("c", False), ("xy", False), ("z", False))
MID = (("c", True), ("xy", False), ("z", False))


def dot(left, right, precision=None):
    return jnp.dot(left, right, preferred_element_type=F32, precision=precision)


def dot_nt(left, right, precision=None):
    return lax.dot_general(
        left, right, (((1,), (1,)), ((), ())), preferred_element_type=F32, precision=precision
    )


def split(values):
    high = values.astype(BF16)
    return high, (values - high.astype(F32)).astype(BF16)


def stack4(values):
    high, low = split(values)
    return jnp.concatenate([high, high, low, low], axis=0)


def lanes_of(shape):
    return lax.broadcasted_iota(jnp.int32, shape, len(shape) - 1)


def high_low(doubled):
    high = doubled.astype(BF16).astype(F32)
    return jnp.where(lanes_of(doubled.shape) < M, high, doubled - high).astype(BF16)


def twice(values):
    return jnp.concatenate([values, values], axis=1)


def pair_rows(values, blocks):
    rows = []
    for block in blocks:
        others = values[8 * block :]
        for i in range(8 * block, 8 * block + 8):
            rows.append(values[i : i + 1] * others)
    return jnp.concatenate(rows, axis=0)


def add_pairs(total_ref, values, weights, first=False):
    for blocks in GROUPS:
        rows = slice(BASES[blocks[0]], BASES[blocks[-1] + 1])
        high, low = split(pair_rows(values, blocks))
        part = dot_nt(high, weights) + dot_nt(low, weights)
        if first:
            total_ref[rows] = part
        else:
            total_ref[rows] += part


def pack(total_ref, small, buffer_ref, scale):
    for at in range(0, HALF, 128):
        top = total_ref[at : at + 128]
        bottom = total_ref[HALF + at : HALF + at + 128]
        top = top + pltpu.roll(top, M, 1)
        bottom = bottom + pltpu.roll(bottom, M, 1)
        buffer_ref[at : at + 128] = jnp.where(lanes_of(top.shape) < M, top, bottom) * scale
    buffer_ref[HALF : HALF + SMALL] = (
        jnp.where(lanes_of((SMALL, 128)) < M, small[:SMALL], small[SMALL:]) * scale
    )
    buffer_ref[HALF + SMALL :] = jnp.zeros((ROWS - HALF - SMALL, 128), F32)


def unpack_rows(packed):
    turned = pltpu.roll(packed, M, 1)
    left = lanes_of(packed.shape) < M
    return jnp.where(left, packed, turned), jnp.where(left, turned, packed)


def unpack_small(packed):
    top, bottom = unpack_rows(packed)
    return jnp.concatenate([top, bottom], axis=0)


def expand(buffer_ref, pairs_ref, full_ref):
    for at in range(0, HALF, 128):
        top, bottom = unpack_rows(buffer_ref[at : at + 128])
        pairs_ref[at : at + 128] = top
        pairs_ref[HALF + at : HALF + at + 128] = bottom
    for i in range(M):
        block = i // 8
        count = M - 8 * block
        start = BASES[block] + (i - 8 * block) * count
        full_ref[i * M + 8 * block : (i + 1) * M] = pairs_ref[start : start + count]
        for below in range(block):
            stride = M - 8 * below
            start = BASES[below] + i - 8 * below
            full_ref[i * M + 8 * below : i * M + 8 * below + 8] = pairs_ref[
                pl.ds(start, 8, stride=stride), :
            ]


def contract(parts_ref, stacked, factors, total):
    for chunk in range(8):
        left = parts_ref[chunk * 512 : (chunk + 1) * 512]
        inner = dot(twice(left), stacked)
        for i in range(8):
            at = chunk * 8 + i
            total = total + inner[i * M : (i + 1) * M] * factors[at : at + 1]
    return total


def gram_of(parts, others):
    full = dot_nt(parts, others)
    half = full[:M] + full[M:]
    return half + pltpu.roll(half, M, 1)


def identity_matrix():
    row = lax.broadcasted_iota(jnp.int32, (M, M), 0)
    return jnp.where(row == lanes_of((M, M)), 1.0, 0.0).astype(F32)


def inverse_factor(gram):
    row = lax.broadcasted_iota(jnp.int32, (M, 2 * M), 0)
    lane = lanes_of((M, 2 * M))
    table = jnp.where(lane < M, gram, jnp.where(lane - M == row, 1.0, 0.0))
    done = []
    for block in range(M // 8):
        height = M - 8 * block
        row = lax.broadcasted_iota(jnp.int32, (height, 2 * M), 0)
        columns = [
            jnp.broadcast_to(table[:, 8 * block + j : 8 * block + j + 1], (height, 2 * M))
            for j in range(8)
        ]
        head, tail = table[:8], table[8:]
        scales = jnp.zeros((8, 2 * M), F32)
        for j in range(8):
            pivot = columns[j][j : j + 1]
            factor = jnp.where(row > j, columns[j] * (1.0 / pivot), 0.0)
            scales = jnp.where(row[:8] == j, lax.rsqrt(pivot), scales)
            pivot_row = head[j : j + 1]
            for later in range(j + 1, 8):
                columns[later] = columns[later] - factor * columns[later][j : j + 1]
            head = head - factor[:8] * pivot_row
            if height > 8:
                tail = tail - factor[8:] * pivot_row
        done.append(head * scales)
        table = tail
    return pltpu.roll(jnp.concatenate(done, axis=0), M, 1)


def kernel(cells, samples, modes_ref, mean_ref, coef_ref, out_modes, out_mean, out_coef, *scratch):
    (field, grad, linear, field_hl, force_hl, step_hl, centered, pair_sum, pairs, full_t, full_q,
     t_parts, q_parts, q_high, q_low, halo_send, halo_recv, halo_ssem, halo_rsem,
     mean_buf, t_buf, q_buf, gram_buf, t_all, q_all, gram_all) = scratch[:26]
    refs = scratch[26:]
    place = coordinates()
    gx, gy = lax.axis_index("gx"), lax.axis_index("gy")
    barrier = pltpu.get_barrier_semaphore()
    around = [((gx + 1) % 8, gy), ((gx + 7) % 8, gy), (gx, (gy + 1) % 32), (gx, (gy + 31) % 32)]
    count = 0
    for axes in ("c", "xy", "z"):
        n, me = group_size(axes), own_member(axes, place)
        for offset in range(1, n):
            pl.semaphore_signal(
                barrier, inc=1, device_id=member_id(axes, (me + offset) % n, place), device_id_type=MESH
            )
            count += 1
    for neighbour in around:
        pl.semaphore_signal(barrier, inc=1, device_id=neighbour, device_id_type=MESH)
        count += 1

    reducers = []
    at = 0
    for buffer, result, stages in (
        (mean_buf, mean_buf, TINY),
        (t_buf, t_all, BIG),
        (q_buf, q_all, BIG),
        (gram_buf, gram_all, MID),
    ):
        shapes = AllReduce.scratch(buffer.shape[0], stages)
        reducers.append(AllReduce(place, buffer, result, stages, refs[at : at + len(shapes)]))
        at += len(shapes)
    mean_sum, t_sum, q_sum, gram_sum = reducers

    eye = lax.broadcasted_iota(jnp.int32, (M, 128), 0) == lanes_of((M, 128))
    sums = jnp.sum(coef_ref[...], axis=1, keepdims=True)
    mean_buf[...] = jnp.broadcast_to(
        jnp.sum(jnp.where(eye, sums, 0.0), axis=0, keepdims=True), (8, 128)
    )

    rows = 72
    lane = lanes_of((rows, 128))
    first = jnp.zeros((rows, 128), F32)
    last = jnp.zeros((rows, 128), F32)
    for y in range(16):
        modes = modes_ref[pl.ds(y, M, stride=16), :]
        field[y, :M] = modes
        high, low = split(modes)
        side = slice(128 * (y % 2), 128 * (y % 2) + 128)
        field_hl[y // 2, :M, side] = high
        field_hl[y // 2, M:, side] = low
        field[y, M:] = jnp.broadcast_to(mean_ref[y : y + 1], (8, 128))
        here = field[y]
        first = jnp.where(lane == y, pltpu.roll(here, y, 1) if y else here, first)
        last = jnp.where(lane == y, pltpu.roll(here, y + 1, 1), last)
        inner = 2.0 * here - jnp.where(lane == 0, 0.0, pltpu.roll(here, 1, 1))
        if y:
            inner = inner - field[y - 1]
        grad[y] = inner
    halo_send[0] = last
    halo_send[1] = first
    halo_send[2] = field[15]
    halo_send[3] = field[0]

    def wide(ref, t):
        return jnp.concatenate([ref[2 * t, :M], ref[2 * t + 1, :M]], axis=1)

    def triad_step(t, carry):
        add_pairs(pair_sum, wide(field, t), jnp.concatenate(split(wide(grad, t)), axis=0))
        return carry

    pair_sum[...] = jnp.zeros(pair_sum.shape, F32)
    lax.fori_loop(0, 3, triad_step, 0)

    pl.semaphore_wait(barrier, count)
    mean_sum.start()
    halos = []
    for side in range(4):
        copy = pltpu.make_async_remote_copy(
            src_ref=halo_send.at[side],
            dst_ref=halo_recv.at[side],
            send_sem=halo_ssem.at[side],
            recv_sem=halo_rsem.at[side],
            device_id=around[side],
            device_id_type=MESH,
        )
        copy.start()
        halos.append(copy)
    lax.fori_loop(3, 4, triad_step, 0)
    mean_sum.advance()
    lax.fori_loop(4, 8, triad_step, 0)

    for copy in halos:
        copy.wait_recv()
    for copy in halos:
        copy.wait_send()
    mean_sum.advance()
    west, east, south, north = halo_recv[0], halo_recv[1], halo_recv[2], halo_recv[3]
    edge = jnp.concatenate([field[0, :M], first[:M]], axis=1)
    beyond = jnp.concatenate([south[:M], jnp.where(lane < 16, west, 0.0)[:M]], axis=1)
    add_pairs(pair_sum, edge, jnp.concatenate(split(-beyond), axis=0))
    coupling = jnp.zeros((M, 128), F32)
    for y in range(16):
        here = field[y]
        from_west = pltpu.roll(west, (128 - y) % 128, 1) if y else west
        from_east = pltpu.roll(east, 127 - y, 1)
        below = field[y - 1] if y else south
        above = field[y + 1] if y < 15 else north
        left = jnp.where(lane == 0, from_west, pltpu.roll(here, 1, 1))
        right = jnp.where(lane == 127, from_east, pltpu.roll(here, 127, 1))
        up = 2.0 * here - left - below
        lap = left + right + below + above - 4.0 * here
        grad[y] = up
        mean = mean_ref[y : y + 1]
        mean_up = up[M : M + 1]
        line = -mean * up[:M] - here[:M] * mean_up + VISCOSITY * lap[:M]
        linear[y] = line
        out_mean[y : y + 1] = mean + TIME_STEP * (-mean * mean_up + VISCOSITY * lap[M : M + 1])
    for t in range(8):
        line_hl = jnp.concatenate(split(wide(linear, t)), axis=0)
        coupling = coupling + gram_of(field_hl[t], line_hl)
    pack(pair_sum, -coupling, q_buf, -1.0 / cells)
    q_sum.start()
    mean_sum.finish()

    sample_mean = jnp.sum(jnp.where(eye, mean_buf[0:1], 0.0), axis=1, keepdims=True) / samples
    centered[...] = coef_ref[...] - sample_mean
    q_sum.advance()
    second = jnp.zeros((M, 128), F32)
    for t in range(2):
        values = centered[:, 256 * t : 256 * t + 256]
        values_hl = jnp.concatenate(split(values), axis=0)
        add_pairs(pair_sum, values, values_hl, first=t == 0)
        second = second + gram_of(values_hl, values_hl)
    pack(pair_sum, second, t_buf, 1.0 / samples)
    t_sum.start()
    q_sum.advance()
    t_sum.advance()
    q_sum.advance()
    t_sum.advance()
    q_sum.advance()
    t_sum.advance()
    q_sum.finish()
    expand(q_all, pairs, full_q)
    for j in range(M):
        at = slice(j * M, (j + 1) * M)
        q_values = full_q[at]
        high, low = split(q_values)
        q_high[at] = high
        q_low[at] = low
        q_parts[at] = high_low(q_values)
    coupled = unpack_small(q_all[HALF : HALF + SMALL])
    t_sum.drain()

    covariance = unpack_small(t_all[HALF : HALF + SMALL])
    expand(t_all, pairs, full_t)
    for j in range(M):
        at = slice(j * M, (j + 1) * M)
        t_parts[at] = high_low(full_t[at])
    covariance_parts = twice(high_low(covariance))

    square = jnp.where(lanes_of((M, 128)) < M, covariance * covariance, 0.0)
    square = jnp.sum(jnp.sum(square, axis=1, keepdims=True), axis=0, keepdims=True)
    scaling = jnp.sqrt(square + 1e-06)
    identity = identity_matrix()

    def force_step(t, carry):
        projection, current, inverse = carry
        high, low = field_hl[t, :M], field_hl[t, M:]
        stacked = jnp.concatenate([high, high, low, low], axis=0)
        slope = wide(grad, t)
        moment = contract(t_parts, stacked, slope, jnp.zeros((M, 256), F32))
        forcing = dot(covariance_parts, stack4(wide(linear, t))) - moment
        high, low = split(forcing)
        force_hl[t, :M] = high
        force_hl[t, M:] = low
        mixed = dot(covariance_parts, stacked) * slope
        row = TIME_STEP * jnp.sum(mixed, axis=0, keepdims=True)
        out_mean[pl.ds(2 * t, 1)] += -row[:, :128]
        out_mean[pl.ds(2 * t + 1, 1)] += -row[:, 128:]

        lefts, rights = [], []
        for k in range(8):
            at = pl.ds(pl.multiple_of((8 * t + k) * M, M), M)
            lefts += [t_parts[at]] * 2
            rights += [q_high[at], q_low[at]]
        projection = projection + dot_nt(
            jnp.concatenate(lefts, axis=1), jnp.concatenate(rights, axis=1)
        )

        middle = 0.5 * (3.0 * identity - dot(inverse, current, HIGHEST))
        live = t < NS_ITERS
        next_current = jnp.where(live, dot(current, middle, HIGHEST), current)
        next_inverse = jnp.where(live, dot(middle, inverse, HIGHEST), inverse)
        return projection, next_current, next_inverse

    start = covariance[:, :M] / scaling
    projection, current, inverse = lax.fori_loop(
        0, 8, force_step, (jnp.zeros((M, M), F32), start, identity)
    )
    projection = projection + dot_nt(covariance[:, :M], coupled[:, :M], HIGHEST)
    half_power = inverse / jnp.sqrt(scaling)
    weighting = dot(half_power, half_power, HIGHEST)
    mixed = dot(weighting, projection, HIGHEST)
    step_parts = jnp.concatenate(
        [twice(high_low(twice(weighting))), twice(high_low(twice(-mixed)))], axis=1
    )
    gram = jnp.zeros((M, 128), F32)
    for t in range(8):
        high, low = force_hl[t, :M], force_hl[t, M:]
        mode_high, mode_low = field_hl[t, :M], field_hl[t, M:]
        stacked = jnp.concatenate(
            [high, high, low, low, mode_high, mode_high, mode_low, mode_low], axis=0
        )
        stepped = wide(field, t) + TIME_STEP * dot(step_parts, stacked)
        high, low = split(stepped)
        step_hl[t, :M] = high
        step_hl[t, M:] = low
        both = jnp.concatenate([high, low], axis=0)
        gram = gram + gram_of(both, both)
    gram_buf[...] = jnp.where(lanes_of((SMALL, 128)) < M, gram[:SMALL], gram[SMALL:]) * (1.0 / cells)
    gram_sum.start()

    constant = jnp.zeros((M, 128), F32)
    for j in range(M):
        constant = constant + full_q[j * M : (j + 1) * M] * covariance[j : j + 1]
    constant = jnp.sum(jnp.where(lanes_of((M, 128)) < M, constant, 0.0), axis=1, keepdims=True)
    coupled_parts = twice(high_low(coupled))
    for t in range(2):
        if t:
            gram_sum.advance()
        values = centered[:, 256 * t : 256 * t + 256]
        stacked = stack4(values)
        total = contract(q_parts, stacked, values, dot(coupled_parts, stacked)) - constant
        out_coef[:, 256 * t : 256 * t + 256] = values + TIME_STEP * total

    gram_sum.drain()
    factor = inverse_factor(unpack_small(gram_all[...]))
    factor_parts = twice(high_low(jnp.where(lanes_of((M, 128)) < M, factor, pltpu.roll(factor, M, 1))))
    for t in range(8):
        high, low = step_hl[t, :M], step_hl[t, M:]
        result = dot(factor_parts, jnp.concatenate([high, high, low, low], axis=0))
        out_modes[pl.ds(2 * t, M, stride=16), :] = result[:, :128]
        out_modes[pl.ds(2 * t + 1, M, stride=16), :] = result[:, 128:]


def per_device(mode_fields, mean_field, coefficients):
    devices = lax.axis_size("gx") * lax.axis_size("gy")
    cells = mode_fields.shape[1] * mode_fields.shape[2] * devices
    samples = coefficients.shape[1] * devices
    scratch = [
        pltpu.VMEM((16, 72, 128), F32),
        pltpu.VMEM((16, 72, 128), F32),
        pltpu.VMEM((16, M, 128), F32),
        pltpu.VMEM((8, 128, 256), BF16),
        pltpu.VMEM((8, 128, 256), BF16),
        pltpu.VMEM((8, 128, 256), BF16),
        pltpu.VMEM((M, 512), F32),
        pltpu.VMEM((PAIRS, 128), F32),
        pltpu.VMEM((PAIRS, 128), F32),
        pltpu.VMEM((M * M, 128), F32),
        pltpu.VMEM((M * M, 128), F32),
        pltpu.VMEM((M * M, 128), BF16),
        pltpu.VMEM((M * M, 128), BF16),
        pltpu.VMEM((M * M, 128), BF16),
        pltpu.VMEM((M * M, 128), BF16),
        pltpu.VMEM((4, 72, 128), F32),
        pltpu.VMEM((4, 72, 128), F32),
        pltpu.SemaphoreType.DMA((4,)),
        pltpu.SemaphoreType.DMA((4,)),
        pltpu.VMEM((8, 128), F32),
        pltpu.VMEM((ROWS, 128), F32),
        pltpu.VMEM((ROWS, 128), F32),
        pltpu.VMEM((SMALL, 128), F32),
        pltpu.VMEM((ROWS, 128), F32),
        pltpu.VMEM((ROWS, 128), F32),
        pltpu.VMEM((SMALL, 128), F32),
    ]
    for size, stages in ((8, TINY), (ROWS, BIG), (ROWS, BIG), (SMALL, MID)):
        scratch += AllReduce.scratch(size, stages)
    whole = pl.BlockSpec(memory_space=pltpu.VMEM)
    fields, new_mean, new_coefficients = pl.pallas_call(
        functools.partial(kernel, cells, samples),
        out_shape=(
            jax.ShapeDtypeStruct((16 * M, 128), F32),
            jax.ShapeDtypeStruct(mean_field.shape, F32),
            jax.ShapeDtypeStruct(coefficients.shape, F32),
        ),
        in_specs=[whole] * 3,
        out_specs=(whole,) * 3,
        scratch_shapes=scratch,
        compiler_params=pltpu.CompilerParams(
            collective_id=0, has_side_effects=True, vmem_limit_bytes=56 * 2**20
        ),
    )(mode_fields.reshape(16 * M, 128), mean_field, coefficients)
    return fields.reshape(mode_fields.shape), new_mean, new_coefficients


def solution(mesh):
    placed = (P(None, "gy", "gx"), P("gy", "gx"), P(None, ("gx", "gy")))
    return jax.shard_map(
        per_device, mesh=mesh, in_specs=placed, out_specs=placed, check_vma=False
    )
```
